256 devices in a mesh: rows: 8 (over y, core), cols: 8 (over z), seg: 4 (over x).
Axes of the slice: x: 4, y: 4, z: 8, core: 2. Of those that a mesh axis runs over, the one named last changes fastest.
Arguments:
- right_side: float32 [64, 65536], P(None, ('rows', 'seg'))
- near_blocks: bfloat16 [8, 4, 8, 16, 128, 128], P('rows', 'seg', 'cols'), may hold values from -0.1875 to 0.1875
- near_rows: int32 [8, 4, 8, 16], P('rows', 'seg', 'cols'), may hold values from 0 to 15
- near_cols: int32 [8, 4, 8, 16], P('rows', 'seg', 'cols'), may hold values from 0 to 63
- left_factors: bfloat16 [8, 4, 8, 256, 64, 128], P('rows', 'seg', 'cols'), may hold values from -0.0625 to 0.0625
- right_factors: bfloat16 [8, 4, 8, 256, 64, 128], P('rows', 'seg', 'cols'), may hold values from -0.5 to 0.5
- slot_ranks: int32 [8, 4, 8, 256], P('rows', 'seg', 'cols'), may hold values from 0 to 64, as said below
- slot_rows: int32 [8, 4, 8, 256], P('rows', 'seg', 'cols'), may hold values from 0 to 15
- slot_cols: int32 [8, 4, 8, 256], P('rows', 'seg', 'cols'), may hold values from 0 to 63
Outputs:
- solution: float32 [64, 65536], P(None, ('rows', 'seg'))
- hessen: float32 [192, 128], replicated
The draws below stay inside these ranges and needn't reach their ends.
Inputs may be any that keep to these rules, and one draw needn't show every extreme that they name: `slot_ranks`: 0 marks an unused slot; the used slots of a device come first and hold ranks of 16 or more; slot 0 has rank 64 on every device.
All inputs are finite; a program needn't handle non-finite values.
Results may differ from the reference program's by a relative error of at most 0.0013.
Values may be sent and summed in bfloat16 or wider, within the bound.
No kernel may reach another device: no remote copies, remote signals or barrier semaphores. Data moves between devices by JAX's collectives and lax.ppermute only.
A program may use at most 64 MiB of HBM per device.

```python
import math
import jax
import jax.numpy as jnp
from jax import lax

CS = 128
KMAX = 64
R = 64
CL_DEV = 16
LR_DEV = 256
NF_DEV = 16
N = 65536
COLCL = 64
N_ROWS = 8
N_COLS = 8
N_SEG = 4


def draw_right_side(key, part):
    key = jax.random.fold_in(key, 11)
    keys = jax.random.split(key, 3)
    position = jnp.arange(N, dtype=jnp.float32) / N
    row_scale = 0.2 * jnp.exp(jax.random.uniform(keys[0], (1, N), minval=0.0, maxval=math.log(10.0)) + position[None, :] * math.log(3.0))
    col_scale = jnp.exp(jax.random.uniform(keys[1], (R, 1), minval=math.log(0.3), maxval=math.log(3.0)))
    values = jax.random.normal(keys[2], (R, N))
    return (values * row_scale * col_scale).astype(jnp.float32)


def draw_slot_ranks(key, part):
    key = jax.random.fold_in(key, 23)
    keys = jax.random.split(key, 3)
    pieces = N_ROWS * N_SEG
    shifts = jax.random.randint(keys[0], (pieces,), 0, 4)
    full_at = jax.random.randint(keys[1], (), 0, pieces)
    places = jnp.arange(pieces, dtype=jnp.int32)
    shifts = jnp.where(places == full_at, 0, shifts)
    shifts = jnp.where(places == (full_at + 1) % pieces, 3, shifts)
    used = LR_DEV // jnp.left_shift(jnp.int32(1), shifts)
    ranks = jax.random.randint(keys[2], (pieces, N_COLS, LR_DEV), KMAX // 4, KMAX + 1)
    slots = jnp.arange(LR_DEV, dtype=jnp.int32)
    ranks = jnp.where(slots[None, None, :] == 0, KMAX, ranks)
    ranks = jnp.where(slots[None, None, :] < used[:, None, None], ranks, 0)
    return ranks.reshape(N_ROWS, N_SEG, N_COLS, LR_DEV).astype(jnp.int32)


def plant(drawn, key, least, high):
    spot = [jax.random.randint(jax.random.fold_in(key, axis), (), 0, length) for axis, length in enumerate(drawn.shape)]
    longest = drawn.shape.index(max(drawn.shape))
    neighbour = spot[:longest] + [(spot[longest] + 1) % drawn.shape[longest]] + spot[longest + 1:]
    return drawn.at[tuple(spot)].set(least).at[tuple(neighbour)].set(high)


def block_levels(own_key, shape, cuts, low, top_value):
    def one(axis_at, shards_of):
        heights = jax.random.uniform(jax.random.fold_in(jax.random.fold_in(own_key, 6), axis_at), (shards_of,), jnp.float32, low / len(cuts), top_value / len(cuts))
        return jnp.repeat(jnp.exp(heights), shape[axis_at] // shards_of).reshape((-1,) + (1,) * (len(shape) - axis_at - 1))

    factor_of = one(*cuts[0])
    for cut in cuts[1:]:
        factor_of = factor_of * one(*cut)
    return factor_of


def bell_draw(stream_key, extent, spread, most, cuts=(), held_as=jnp.bfloat16):
    gain = block_levels(stream_key, extent, cuts, -0.22, 0.18) if cuts else 1.0
    result = jax.random.normal(stream_key, extent, jnp.float32) * spread * gain
    return jnp.minimum(jnp.maximum(result, -most), most).astype(held_as)


def setup_inputs(seed: int = 0) -> dict:
    seeds = jax.random.split(jax.random.key(seed), 10)
    return {
        "right_side": draw_right_side(jax.random.fold_in(seeds[9], 71), 0),
        "near_blocks": bell_draw(seeds[1], (N_ROWS, N_SEG, N_COLS, NF_DEV, CS, CS), (CS * NF_DEV * N_COLS // CL_DEV) ** -0.5, 0.1875, ((0, 8), (1, 4), (2, 8))),
        "near_rows": plant(jax.random.randint(seeds[2], (N_ROWS, N_SEG, N_COLS, NF_DEV), 0, CL_DEV), jax.random.fold_in(seeds[2], 1), 0, CL_DEV - 1).astype(jnp.int32),
        "near_cols": plant(jax.random.randint(seeds[3], (N_ROWS, N_SEG, N_COLS, NF_DEV), 0, COLCL), jax.random.fold_in(seeds[3], 1), 0, COLCL - 1).astype(jnp.int32),
        "left_factors": bell_draw(seeds[4], (N_ROWS, N_SEG, N_COLS, LR_DEV, KMAX, CS), (KMAX * LR_DEV * N_COLS // CL_DEV) ** -0.5, 0.0625, ((0, 8), (1, 4), (2, 8))),
        "right_factors": bell_draw(seeds[5], (N_ROWS, N_SEG, N_COLS, LR_DEV, KMAX, CS), CS ** -0.5, 0.5, ((0, 8), (1, 4), (2, 8))),
        "slot_ranks": draw_slot_ranks(jax.random.fold_in(seeds[9], 71), 0),
        "slot_rows": plant(jax.random.randint(seeds[7], (N_ROWS, N_SEG, N_COLS, LR_DEV), 0, CL_DEV), jax.random.fold_in(seeds[7], 1), 0, CL_DEV - 1).astype(jnp.int32),
        "slot_cols": plant(jax.random.randint(seeds[8], (N_ROWS, N_SEG, N_COLS, LR_DEV), 0, COLCL), jax.random.fold_in(seeds[8], 1), 0, COLCL - 1).astype(jnp.int32),
    }


FULL_PRECISION = lax.Precision.HIGHEST

def inner_gram(first_set, second_set):
    return jnp.einsum('ai,bi->ab', first_set, second_set, precision=FULL_PRECISION)

def combine(coeffs, vectors):
    return jnp.einsum('ab,ai->bi', coeffs, vectors, precision=FULL_PRECISION)

def square_of(matrix):
    return jnp.einsum('ab,ac->bc', matrix, matrix, precision=FULL_PRECISION)

def cholesky_upper(gram):
    order = gram.shape[0]
    places = lax.broadcasted_iota(jnp.int32, (order,), 0)

    def step_one(column, carry):
        work, upper = carry
        pivot_row = lax.dynamic_slice_in_dim(work, column, 1, 0)[0]
        pivot = lax.dynamic_slice_in_dim(pivot_row, column, 1, 0)[0]
        scaled = jnp.where(places >= column, pivot_row / jnp.sqrt(pivot), 0.0)
        work = work - scaled[:, None] * scaled[None, :]
        marker = (places == column).astype(gram.dtype)
        upper = upper + marker[:, None] * scaled[None, :]
        return (work, upper)
    return lax.fori_loop(0, order, step_one, (gram, jnp.zeros_like(gram)))[1]

def upper_inverse(upper):
    order = upper.shape[0]
    places = lax.broadcasted_iota(jnp.int32, (order,), 0)

    def step_one(count, inverse):
        index = order - 1 - count
        row_upper = lax.dynamic_slice_in_dim(upper, index, 1, 0)[0]
        diag_value = lax.dynamic_slice_in_dim(row_upper, index, 1, 0)[0]
        beyond = jnp.where(places > index, row_upper, 0.0)
        marker = (places == index).astype(upper.dtype)
        new_row = (marker - jnp.dot(beyond, inverse, precision=FULL_PRECISION)) / diag_value
        return inverse + marker[:, None] * new_row[None, :]
    return lax.fori_loop(0, order, step_one, jnp.zeros_like(upper))

def chol_parts(gram):
    upper = cholesky_upper(gram)
    return (upper, upper_inverse(upper))

def chol_solve(gram, target):
    inverse = upper_inverse(cholesky_upper(gram))
    return jnp.dot(inverse, jnp.dot(inverse.T, target, precision=FULL_PRECISION), precision=FULL_PRECISION)

def block_terms(panel, dense, near_rows, near_cols, left_factors, right_factors, slot_ranks, slot_rows, slot_cols):
    picked = jnp.take(panel, slot_cols, axis=1).astype(jnp.float32)
    coeffs = jnp.einsum('rki,kqi->kqr', picked, right_factors.astype(jnp.float32))
    rank_pos = jnp.arange(KMAX, dtype=jnp.int32)
    usable = rank_pos[None, :] < slot_ranks[:, None]
    coeffs = jnp.where(usable[:, :, None], coeffs, 0.0).astype(jnp.bfloat16)
    low_rank = jnp.einsum('kqr,kqi->kri', coeffs.astype(jnp.float32), left_factors.astype(jnp.float32))
    nearby = jnp.take(panel, near_cols, axis=1).astype(jnp.float32)
    near_part = jnp.einsum('kij,rkj->kri', dense.astype(jnp.float32), nearby)
    targets = jnp.arange(CL_DEV, dtype=jnp.int32)[:, None]
    slot_select = (slot_rows[None, :] == targets).astype(jnp.float32)
    near_select = (near_rows[None, :] == targets).astype(jnp.float32)
    return jnp.einsum('lk,kri->rli', slot_select, low_rank, precision=FULL_PRECISION) + jnp.einsum('lk,kri->rli', near_select, near_part, precision=FULL_PRECISION)

def apply_operator(vectors, near_blocks, near_rows, near_cols, left_factors, right_factors, slot_ranks, slot_rows, slot_cols):
    pieces = N_ROWS * N_SEG
    group = CL_DEV // N_COLS
    cells = vectors.astype(jnp.bfloat16).reshape(R, pieces, N_COLS, group, CS)
    panels = jnp.transpose(cells, (2, 0, 1, 3, 4)).reshape(N_COLS, R, pieces * group, CS)
    operands = tuple((item.reshape((pieces, N_COLS) + item.shape[3:]) for item in (near_blocks, near_rows, near_cols, left_factors, right_factors, slot_ranks, slot_rows, slot_cols)))

    def one_piece(items):
        total = jnp.zeros((R, CL_DEV, CS), jnp.float32)
        for column in range(N_COLS):
            total = total + block_terms(panels[column], *[item[column] for item in items])
        return total
    terms = lax.map(one_piece, operands)
    terms = jnp.transpose(terms, (1, 0, 2, 3)).reshape(R, pieces * CL_DEV * CS)
    return terms + 0.5 * vectors

def reference(right_side, near_blocks, near_rows, near_cols, left_factors, right_factors, slot_ranks, slot_rows, slot_cols):
    operator = (near_blocks, near_rows, near_cols, left_factors, right_factors, slot_ranks, slot_rows, slot_cols)
    start_factor, start_inverse = chol_parts(inner_gram(right_side, right_side))
    first_basis = combine(start_inverse, right_side)
    image = apply_operator(first_basis, *operator)
    head_one = inner_gram(first_basis, image)
    image = image - combine(head_one, first_basis)
    lower_one, lower_inverse = chol_parts(inner_gram(image, image))
    second_basis = combine(lower_inverse, image)
    image = apply_operator(second_basis, *operator)
    cross_one = inner_gram(first_basis, image)
    cross_two = inner_gram(second_basis, image)
    image = image - combine(cross_one, first_basis) - combine(cross_two, second_basis)
    lower_two = cholesky_upper(inner_gram(image, image))
    zero_block = jnp.zeros_like(head_one)
    hessen = jnp.concatenate([jnp.concatenate([head_one, cross_one], 1), jnp.concatenate([lower_one, cross_two], 1), jnp.concatenate([zero_block, lower_two], 1)], 0)
    target = jnp.concatenate([jnp.dot(head_one.T, start_factor, precision=FULL_PRECISION), jnp.dot(cross_one.T, start_factor, precision=FULL_PRECISION)], 0)
    weights = chol_solve(square_of(hessen), target)
    solution = combine(weights[:R], first_basis) + combine(weights[R:], second_basis)
    return (solution, hessen)
```

```python
import functools

import jax
import jax.numpy as jnp
from jax import lax
from jax.experimental import pallas as pl
from jax.experimental.pallas import tpu as pltpu
from jax.sharding import PartitionSpec as P

FULL = lax.Precision.HIGHEST
NN = (((1,), (0,)), ((), ()))
NT = (((1,), (1,)), ((), ()))
TN = (((0,), (0,)), ((), ()))
CHUNKS = 8
UNROLL = 8
VMEM_LIMIT = 48 * 1024 * 1024


def mm(a, b, dims=NN):
    return lax.dot_general(a, b, dims, precision=FULL, preferred_element_type=jnp.float32)


def vmem():
    return pl.BlockSpec(memory_space=pltpu.VMEM)


def smem():
    return pl.BlockSpec(memory_space=pltpu.SMEM)


def eye(order):
    rows = lax.broadcasted_iota(jnp.int32, (order, order), 0)
    cols = lax.broadcasted_iota(jnp.int32, (order, order), 1)
    return (rows == cols).astype(jnp.float32)


def eliminate(works):
    order = works[0].shape[0]
    works = list(works)
    for k in range(order):
        base = (k // 8) * 8
        for at, work in enumerate(works):
            pivot_row = work[k : k + 1, :]
            ratio = pivot_row * (1.0 / pivot_row[:, k : k + 1])
            low = work[base:, :]
            places = lax.broadcasted_iota(jnp.int32, (order - base, 1), 0) + base
            factor = jnp.where(places > k, low[:, k : k + 1], 0.0)
            low = low - factor * ratio
            works[at] = low if base == 0 else jnp.concatenate([work[:base], low], 0)
    results = []
    for work in works:
        rows = lax.broadcasted_iota(jnp.int32, work.shape, 0)
        cols = lax.broadcasted_iota(jnp.int32, work.shape, 1)
        diagonal = jnp.sum(jnp.where(rows == cols, work, 0.0), axis=1, keepdims=True)
        scaled = work * (1.0 / jnp.sqrt(diagonal))
        results.append(jnp.where(cols >= rows, scaled, jnp.where(cols >= order, scaled, 0.0)))
    return results


def start_gram_kernel(piece_ref, gram_ref):
    piece = piece_ref[...]
    gram_ref[...] = mm(piece, piece, NT)


def start_factor_kernel(gram_ref, factor_ref, inverse_ref):
    order = gram_ref.shape[0]
    (done,) = eliminate([jnp.concatenate([gram_ref[...], eye(order)], 1)])
    factor_ref[...] = done[:, :order]
    inverse_ref[...] = done[:, order:]


def share_gram_kernel(count, *refs):
    bases, terms_ref, share_ref, gram_ref = refs[:count], refs[count], refs[count + 1], refs[count + 2]
    share = terms_ref[0]
    for index in range(1, terms_ref.shape[0]):
        share = share + terms_ref[index]
    share_ref[...] = share
    order = share.shape[1]
    for at in range(count + 1):
        total = None
        for half in range(share.shape[0]):
            left = share[half] if at == count else bases[at][half]
            product = mm(left, share[half], NT)
            total = product if total is None else total + product
        gram_ref[at * order : (at + 1) * order, :] = total


def sum_leading(ref):
    total = ref[0]
    for index in range(1, ref.shape[0]):
        total = total + ref[index]
    return total


def middle_kernel(grams_ref, head_ref, lower_ref, first_ref, second_ref):
    totals = sum_leading(grams_ref)
    order = totals.shape[1]
    cross, square = totals[:order], totals[order:]
    gram = square - mm(cross, cross, TN)
    (done,) = eliminate([jnp.concatenate([gram, eye(order)], 1)])
    inverse = done[:, order:]
    head_ref[...] = cross + 0.5 * eye(order)
    lower_ref[...] = done[:, :order]
    first_ref[...] = inverse
    second_ref[...] = -mm(inverse, cross, NT)


def final_kernel(
    grams_ref, start_ref, head_ref, lower_ref, own_ref, mix_ref, base_ref, hessen_ref, w_right_ref, w_image_ref
):
    totals = sum_leading(grams_ref)
    order = totals.shape[1]
    unit = eye(order)
    cross_one = totals[:order]
    inner = totals[order : 2 * order]
    cross_two = inner + 0.5 * unit
    gram = totals[2 * order :] - mm(cross_one, cross_one, TN) - mm(inner, inner, TN)
    start, head, lower = start_ref[...], head_ref[...], lower_ref[...]
    top = mm(head, head, TN) + mm(lower, lower, TN)
    side = mm(head, cross_one, TN) + mm(lower, cross_two, TN)
    corner = mm(cross_one, cross_one, TN) + mm(cross_two, cross_two, TN) + gram
    upper_target = mm(head, start, TN)
    lower_target = mm(cross_one, start, TN)
    pad = jnp.zeros_like(gram)
    top_done, gram_done = eliminate(
        [jnp.concatenate([top, unit, side, upper_target], 1), jnp.concatenate([gram, pad], 1)]
    )
    inverse_top = top_done[:, order : 2 * order]
    bridge = top_done[:, 2 * order : 3 * order]
    part = top_done[:, 3 * order :]
    schur = corner - mm(bridge, bridge, TN)
    (low_done,) = eliminate(
        [jnp.concatenate([schur, unit, lower_target - mm(bridge, part, TN), pad], 1)]
    )
    low_weights = mm(low_done[:, order : 2 * order], low_done[:, 2 * order : 3 * order], TN)
    top_weights = mm(inverse_top, part - mm(bridge, low_weights), TN)
    hessen_ref[:order, :order] = head
    hessen_ref[:order, order:] = cross_one
    hessen_ref[order : 2 * order, :order] = lower
    hessen_ref[order : 2 * order, order:] = cross_two
    hessen_ref[2 * order :, :order] = pad
    hessen_ref[2 * order :, order:] = gram_done[:, :order]
    w_image_ref[...] = mm(low_weights, own_ref[...], TN)
    first = top_weights + mm(mix_ref[...], low_weights, TN)
    w_right_ref[...] = mm(first, base_ref[...], TN)


def solution_kernel(w_right_ref, w_image_ref, right_ref, image_ref, out_ref):
    leaf = image_ref.shape[-1]
    for cluster in range(image_ref.shape[0] * image_ref.shape[1]):
        cells = pl.ds(cluster * leaf, leaf)
        group = image_ref.shape[1]
        out_ref[:, cells] = mm(w_right_ref[...], right_ref[:, cells]) + mm(
            w_image_ref[...], image_ref[cluster // group, cluster % group]
        )


def apply_kernel(
    panels,
    keep_all,
    near_rows_ref,
    near_cols_ref,
    ranks_ref,
    rows_ref,
    cols_ref,
    *refs,
):
    mixes, refs = refs[:panels], refs[panels:]
    panel_refs, refs = refs[: 2 * panels], refs[2 * panels :]
    near_hbm, left_hbm, right_hbm, basis_ref, terms_ref = refs[:5]
    rounded, near, left, right, sems, near_sem = refs[5:]
    slots = left.shape[0]
    per = slots // CHUNKS
    copies = []
    near_copy = pltpu.make_async_copy(near_hbm, near, near_sem)
    near_copy.start()
    for chunk in range(CHUNKS):
        part = pl.ds(chunk * per, per)
        pair = (
            pltpu.make_async_copy(right_hbm.at[part], right.at[part], sems.at[chunk, 0]),
            pltpu.make_async_copy(left_hbm.at[part], left.at[part], sems.at[chunk, 1]),
        )
        for copy in pair:
            copy.start()
        copies.append(pair)
    terms_ref[...] = jnp.zeros_like(terms_ref)
    half_count = panel_refs[0].shape[0]
    group = terms_ref.shape[1]
    coeffs = [mix[...] for mix in mixes]
    for side in range(2):
        offset = side * half_count

        def make_basis(index, _, side=side, offset=offset):
            value = mm(coeffs[0], panel_refs[side][index])
            for at in range(1, panels):
                value = value + mm(coeffs[at], panel_refs[2 * at + side][index])
            rounded[offset + index] = value.astype(jnp.bfloat16)
            if keep_all:
                basis_ref[offset + index] = value
            elif side == 0:

                @pl.when(index < group)
                def _():
                    basis_ref[index] = value

            return 0

        lax.fori_loop(0, half_count, make_basis, 0, unroll=4)

    near_copy.wait()
    order = rounded.shape[1]
    columns = lax.broadcasted_iota(jnp.int32, (order, left.shape[1]), 1)

    def add_to(row, value):
        terms_ref[row // group, row % group] += value

    def near_step(step, _):
        values = []
        for inner in range(4):
            at = step * 4 + inner
            values.append(
                lax.dot_general(
                    rounded[near_cols_ref[at]], near[at], NT, preferred_element_type=jnp.float32
                )
            )
        for inner, value in enumerate(values):
            add_to(near_rows_ref[step * 4 + inner], value)
        return 0

    lax.fori_loop(0, near.shape[0] // 4, near_step, 0)

    def slot_step(step, _):
        coefs = []
        for inner in range(UNROLL):
            at = step * UNROLL + inner
            coef = lax.dot_general(
                rounded[cols_ref[at]], right[at], NT, preferred_element_type=jnp.float32
            )
            coefs.append(jnp.where(columns < ranks_ref[at], coef, 0.0).astype(jnp.bfloat16))
        values = []
        for inner in range(UNROLL):
            values.append(
                lax.dot_general(
                    coefs[inner], left[step * UNROLL + inner], NN, preferred_element_type=jnp.float32
                )
            )
        for inner, value in enumerate(values):
            add_to(rows_ref[step * UNROLL + inner], value)
        return 0

    for chunk in range(CHUNKS):
        for copy in copies[chunk]:
            copy.wait()
        lax.fori_loop(chunk * per // UNROLL, (chunk + 1) * per // UNROLL, slot_step, 0)


def apply_operator(mixes, halves, operator, keep_all, shape_of_terms):
    near, near_rows, near_cols, left, right, ranks, rows, cols = operator
    order, leaf = shape_of_terms[2], shape_of_terms[3]
    clusters = 2 * halves[0].shape[0]
    kept = clusters if keep_all else shape_of_terms[1]
    operands = [near_rows, near_cols, ranks, rows, cols, *mixes, *halves, near, left, right]
    specs = [smem()] * 5 + [vmem()] * (len(mixes) + len(halves)) + [pl.BlockSpec(memory_space=pl.ANY)] * 3
    return pl.pallas_call(
        functools.partial(apply_kernel, len(mixes), keep_all),
        out_shape=(
            jax.ShapeDtypeStruct((kept, order, leaf), jnp.float32),
            jax.ShapeDtypeStruct(shape_of_terms, jnp.float32),
        ),
        in_specs=specs,
        out_specs=(vmem(), vmem()),
        scratch_shapes=[
            pltpu.VMEM((clusters, order, leaf), jnp.bfloat16),
            pltpu.VMEM(near.shape, near.dtype),
            pltpu.VMEM(left.shape, left.dtype),
            pltpu.VMEM(right.shape, right.dtype),
            pltpu.SemaphoreType.DMA((CHUNKS, 2)),
            pltpu.SemaphoreType.DMA,
        ],
        compiler_params=pltpu.CompilerParams(vmem_limit_bytes=VMEM_LIMIT),
    )(*operands)


def call(kernel, outs, *operands):
    return pl.pallas_call(
        kernel,
        out_shape=tuple(jax.ShapeDtypeStruct(shape, jnp.float32) for shape in outs),
        in_specs=[vmem()] * len(operands),
        out_specs=tuple(vmem() for _ in outs),
        compiler_params=pltpu.CompilerParams(vmem_limit_bytes=VMEM_LIMIT),
    )(*operands)


def exchange(values, axis, distance):
    count = lax.axis_size(axis)
    return lax.ppermute(values, axis, [(at, at ^ distance) for at in range(count)])


SEG_STEPS = ("seg", (1, 2, 3))
CHIP_STEPS = ("rows", (2, 4, 6))


def reduce_rows_seg(values):
    for axis, steps in (SEG_STEPS, CHIP_STEPS):
        one, two, three = [exchange(values, axis, step) for step in steps]
        values = (values + one) + (two + three)
    return values + exchange(values, "rows", 1)


def gather_halves(share):
    for axis, steps in (SEG_STEPS, CHIP_STEPS):
        share = jnp.concatenate([share] + [exchange(share, axis, step) for step in steps], 0)
    return [share, exchange(share, "rows", 1)]


def spread_cols(values):
    count = lax.axis_size("cols")
    return lax.all_to_all(jnp.broadcast_to(values[None], (count,) + values.shape), "cols", 0, 0)


def body(
    right_side,
    near_blocks,
    near_rows,
    near_cols,
    left_factors,
    right_factors,
    slot_ranks,
    slot_rows,
    slot_cols,
):
    col_count = lax.axis_size("cols")
    col_index = lax.axis_index("cols")
    order, cells = right_side.shape
    leaf = near_blocks.shape[-1]
    group = cells // leaf // col_count
    me = lax.axis_index("rows") * lax.axis_size("seg") + lax.axis_index("seg")

    def relative(columns):
        piece = (columns.reshape(-1) // group) ^ me
        place = ((piece >> 3) & 3) * 4 + ((piece >> 2) & 1) * 16 + (piece & 3)
        return place * group + columns.reshape(-1) % group

    operator = (
        near_blocks.reshape(near_blocks.shape[3:]),
        near_rows.reshape(-1),
        relative(near_cols),
        left_factors.reshape(left_factors.shape[3:]),
        right_factors.reshape(right_factors.shape[3:]),
        slot_ranks.reshape(-1),
        slot_rows.reshape(-1),
        relative(slot_cols),
    )
    square = (order, order)
    share_shape = (group, order, leaf)
    terms_shape = (col_count,) + share_shape

    share = lax.dynamic_slice_in_dim(right_side, col_index * group * leaf, group * leaf, 1)
    share = jnp.transpose(share.reshape(order, group, leaf), (1, 0, 2))
    start_halves = gather_halves(share)
    (gram,) = call(start_gram_kernel, [square], right_side)
    gram = reduce_rows_seg(gram)
    start_factor, base = call(start_factor_kernel, [square, square], gram)

    first_panel, terms = apply_operator([base], start_halves, operator, True, terms_shape)
    first_share = first_panel[:group]
    received = lax.all_to_all(terms, "cols", 0, 0)
    image, grams = call(
        functools.partial(share_gram_kernel, 1), [share_shape, (2 * order, order)], first_share, received
    )
    image_halves = gather_halves(image)
    image_piece = spread_cols(image)
    grams = spread_cols(reduce_rows_seg(grams))
    head, lower, own, mix = call(middle_kernel, [square] * 4, grams)

    half = first_panel.shape[0] // 2
    second_share, terms = apply_operator(
        [own, mix], image_halves + [first_panel[:half], first_panel[half:]], operator, False, terms_shape
    )
    received = lax.all_to_all(terms, "cols", 0, 0)
    _, grams = call(
        functools.partial(share_gram_kernel, 2),
        [share_shape, (3 * order, order)],
        first_share,
        second_share,
        received,
    )
    grams = spread_cols(reduce_rows_seg(grams))
    hessen, w_right, w_image = call(
        final_kernel,
        [(3 * order, 2 * order), square, square],
        grams,
        start_factor,
        head,
        lower,
        own,
        mix,
        base,
    )
    (answer,) = call(solution_kernel, [(order, cells)], w_right, w_image, right_side, image_piece)
    return (answer, hessen)


def solution(mesh):
    in_specs = (
        P(None, ("rows", "seg")),
        P("rows", "seg", "cols", None, None, None),
        P("rows", "seg", "cols", None),
        P("rows", "seg", "cols", None),
        P("rows", "seg", "cols", None, None, None),
        P("rows", "seg", "cols", None, None, None),
        P("rows", "seg", "cols", None),
        P("rows", "seg", "cols", None),
        P("rows", "seg", "cols", None),
    )
    out_specs = (P(None, ("rows", "seg")), P())
    return jax.shard_map(body, mesh=mesh, in_specs=in_specs, out_specs=out_specs, check_vma=False)
```

```python
import functools

import jax
import jax.numpy as jnp
from jax import lax
from jax.experimental import pallas as pl
from jax.experimental.pallas import tpu as pltpu
from jax.sharding import PartitionSpec as P

FULL = lax.Precision.HIGHEST
NN = (((1,), (0,)), ((), ()))
NT = (((1,), (1,)), ((), ()))
TN = (((0,), (0,)), ((), ()))
CHUNKS = 8
UNROLL = 32
VMEM_LIMIT = 48 * 1024 * 1024


def mm(a, b, dims=NN):
    return lax.dot_general(a, b, dims, precision=FULL, preferred_element_type=jnp.float32)


def vmem():
    return pl.BlockSpec(memory_space=pltpu.VMEM)


def smem():
    return pl.BlockSpec(memory_space=pltpu.SMEM)


def eye(order):
    rows = lax.broadcasted_iota(jnp.int32, (order, order), 0)
    cols = lax.broadcasted_iota(jnp.int32, (order, order), 1)
    return (rows == cols).astype(jnp.float32)


def eliminate(works):
    order = works[0].shape[0]
    groups = [[work[at : at + 8] for at in range(0, order, 8)] for work in works]
    places = lax.broadcasted_iota(jnp.int32, groups[0][0].shape, 0)

    def lane(value, at):
        return jnp.broadcast_to(value[:, at : at + 1], value.shape)

    def pivots(parts, base):
        head = parts[base // 8]
        rows = [jnp.broadcast_to(head[at : at + 1], head.shape) for at in range(8)]
        corner = [[lane(row, base + at) for at in range(8)] for row in rows]
        steps, ratios, scaled = [], [], []
        for at in range(8):
            inverse = 1.0 / corner[at][at]
            ratio = {later: corner[at][later] * inverse for later in range(at + 1, 8)}
            steps.append(rows[at] * inverse)
            ratios.append(ratio)
            scaled.append(rows[at] * (1.0 / jnp.sqrt(corner[at][at])))
            for later in range(at + 1, 8):
                rows[later] = rows[later] - ratio[later] * rows[at]
                for column in range(later, 8):
                    corner[later][column] = corner[later][column] - ratio[later] * corner[at][column]
        result = scaled[0]
        for at in range(1, 8):
            result = jnp.where(places == at, scaled[at], result)
        return result, steps, ratios

    for base in range(0, order, 8):
        for parts in groups:
            parts[base // 8], steps, ratios = pivots(parts, base)
            for below in range(base // 8 + 1, len(parts)):
                value = parts[below]
                factors = [lane(value, base + at) for at in range(8)]
                for at in range(8):
                    for earlier in range(at):
                        factors[at] = factors[at] - ratios[earlier][at] * factors[earlier]
                for at in range(8):
                    value = value - factors[at] * steps[at]
                parts[below] = value
    results = []
    for parts in groups:
        work = jnp.concatenate(parts, 0)
        rows = lax.broadcasted_iota(jnp.int32, work.shape, 0)
        cols = lax.broadcasted_iota(jnp.int32, work.shape, 1)
        results.append(jnp.where(cols >= rows, work, 0.0))
    return results


def split(value):
    high = value.astype(jnp.bfloat16)
    return high, (value - high.astype(jnp.float32)).astype(jnp.bfloat16)


def sum_leading(ref):
    total = ref[0]
    for index in range(1, ref.shape[0]):
        total = total + ref[index].astype(jnp.float32)
    return total


def start_kernel(column_ref, piece_ref, message_ref):
    piece = piece_ref[...]
    group, leaf = message_ref.shape[0] - 1, message_ref.shape[2]
    for half in range(group):
        first = pl.multiple_of((column_ref[0] * group + half) * leaf, leaf)
        message_ref[half] = piece_ref[:, pl.ds(first, leaf)]
    gram = mm(piece, piece, NT)
    message_ref[group] = jnp.concatenate([gram, jnp.zeros_like(gram)], 1)


def share_products(bases, share):
    group = len(share)
    products = []
    for base in bases + [share]:
        total = mm(base[0], share[0], NT)
        for half in range(1, group):
            total = total + mm(base[half], share[half], NT)
        products.append(total)
    return products


def in_cells(ref):
    parts = [ref[at, half] for at in range(ref.shape[0]) for half in range(ref.shape[1])]
    return jnp.concatenate(parts, 1)


def sum_kernel(terms_ref, share_ref):
    share_ref[...] = sum_leading(terms_ref)


def first_image_kernel(base_ref, right_ref, image_ref, share_ref, message_ref):
    basis = mm(base_ref[...], right_ref[...])
    image = in_cells(image_ref)
    order, group = image.shape[0], share_ref.shape[0]
    products = mm(jnp.concatenate([basis, image], 0), image, NT)
    message_ref[:group] = share_ref[...]
    message_ref[group] = jnp.concatenate([products[:order], products[order:]], 1)


def second_image_kernel(first_ref, second_ref, terms_ref, gram_ref):
    total = terms_ref[0].astype(jnp.float32)
    for index in range(1, terms_ref.shape[0]):
        total = total + terms_ref[index].astype(jnp.float32)
    group, order = total.shape[0], total.shape[1]
    share = [total[half] for half in range(group)]
    bases = [[ref[half] for half in range(group)] for ref in (first_ref, second_ref)]
    one, two, square = share_products(bases, share)
    gram_ref[:order] = jnp.concatenate([one, two], 1)
    gram_ref[order:] = jnp.concatenate([square[: order // 2], square[order // 2 :]], 1)


def merge_kernel(own_ref, one_ref, two_ref, three_ref, out_ref):
    refs = (own_ref, one_ref, two_ref, three_ref)
    count = own_ref.shape[0] - 1
    for at, ref in enumerate(refs):
        out_ref[at * count : (at + 1) * count] = ref[:count]
    out_ref[4 * count] = (own_ref[count] + one_ref[count]) + (two_ref[count] + three_ref[count])


def final_kernel(
    grams_ref,
    start_ref,
    head_ref,
    lower_ref,
    top_inverse_ref,
    own_ref,
    mix_ref,
    base_ref,
    right_ref,
    image_ref,
    out_ref,
    hessen_ref,
):
    totals = sum_leading(grams_ref)
    order = start_ref.shape[0]
    unit = eye(order)
    cross_one = totals[:order, :order]
    inner = totals[:order, order:]
    square = jnp.concatenate([totals[order:, :order], totals[order:, order:]], 0)
    cross_two = inner + 0.5 * unit
    gram = square - mm(cross_one, cross_one, TN) - mm(inner, inner, TN)
    start, head, lower = start_ref[...], head_ref[...], lower_ref[...]
    top_inverse = top_inverse_ref[...]
    side = mm(head, cross_one, TN) + mm(lower, cross_two, TN)
    corner = mm(cross_one, cross_one, TN) + mm(cross_two, cross_two, TN) + gram
    bridge = mm(top_inverse, side)
    part = mm(top_inverse, mm(head, start, TN))
    schur = corner - mm(bridge, bridge, TN)
    rest = mm(cross_one, start, TN) - mm(bridge, part, TN)
    schur_done, gram_done = eliminate(
        [jnp.concatenate([schur, unit], 1), jnp.concatenate([gram, rest], 1)]
    )
    low_inverse = schur_done[:, order:]
    low_weights = mm(low_inverse, mm(low_inverse, rest), TN)
    top_weights = mm(top_inverse, part - mm(bridge, low_weights), TN)
    hessen_ref[:order, :] = jnp.concatenate([head, cross_one], 1)
    hessen_ref[order : 2 * order, :] = jnp.concatenate([lower, cross_two], 1)
    hessen_ref[2 * order :, :] = jnp.concatenate([jnp.zeros_like(head), gram_done[:, :order]], 1)
    for_image = mm(low_weights, own_ref[...], TN)
    for_right = mm(top_weights, base_ref[...], TN) + mm(low_weights, mix_ref[...], TN)
    weights = jnp.concatenate([for_right, for_image], 1)
    out_ref[...] = mm(weights, jnp.concatenate([right_ref[...], in_cells(image_ref)], 0))


def start_mixes(gram_refs, out_refs):
    last = gram_refs[0].shape[0] - 1
    totals = gram_refs[0][last] + gram_refs[1][last]
    order = totals.shape[0]
    (done,) = eliminate([jnp.concatenate([totals[:, :order], eye(order)], 1)])
    factor_ref, base_ref = out_refs
    factor_ref[...] = done[:, :order]
    base_ref[...] = done[:, order:]
    return [done[:, order:]]


def middle_mixes(gram_refs, out_refs):
    last = gram_refs[0].shape[0] - 1
    totals = gram_refs[0][last] + gram_refs[1][last]
    base = gram_refs[2][...]
    order = totals.shape[0]
    unit = eye(order)
    cross, square = totals[:, :order], totals[:, order:]
    gram = square - mm(cross, cross, TN)
    head = cross + 0.5 * unit
    top = mm(head, head, TN) + gram
    done, top_done = eliminate(
        [jnp.concatenate([gram, unit], 1), jnp.concatenate([top, unit], 1)]
    )
    own = done[:, order:]
    mix = -mm(mm(own, cross, NT), base)
    head_ref, lower_ref, top_inverse_ref, own_ref, mix_ref = out_refs
    head_ref[...] = head
    lower_ref[...] = done[:, :order]
    top_inverse_ref[...] = top_done[:, order:]
    own_ref[...] = own
    mix_ref[...] = mix
    return [own, mix]


def apply_kernel(prepare, gram_count, out_count, panels, slots_ref, *refs):
    gram_refs, refs = refs[:gram_count], refs[gram_count:]
    panel_refs, refs = refs[: 2 * panels], refs[2 * panels :]
    near_hbm, left_hbm, right_hbm = refs[:3]
    small_outs, refs = refs[3 : 3 + out_count], refs[3 + out_count :]
    basis_ref, terms_ref = refs[:2]
    total, rounded, near, left, right, sems, near_sem = refs[2:]
    slots = left.shape[0]
    per = slots // CHUNKS
    near_copy = pltpu.make_async_copy(near_hbm, near, near_sem)
    near_copy.start()
    copies = []
    for chunk in range(CHUNKS):
        part = pl.ds(chunk * per, per)
        pair = (
            pltpu.make_async_copy(right_hbm.at[part], right.at[part], sems.at[chunk, 0]),
            pltpu.make_async_copy(left_hbm.at[part], left.at[part], sems.at[chunk, 1]),
        )
        for copy in pair:
            copy.start()
        copies.append(pair)
    total[...] = jnp.zeros_like(total)
    mixes = prepare(gram_refs, small_outs)
    group = total.shape[1]
    for half in range(group):
        share = mm(mixes[0], panel_refs[0][half])
        for at in range(1, panels):
            share = share + mm(mixes[at], panel_refs[2 * at][half])
        basis_ref[half] = share
    high, low = split(jnp.concatenate(mixes, 1))
    weights = jnp.concatenate([high, high, low], 1)
    half_count = rounded.shape[0] // 2
    for side in range(2):

        def make_basis(index, _, side=side):
            stacked = jnp.concatenate([panel_refs[2 * at + side][index] for at in range(panels)], 0)
            upper, under = split(stacked)
            value = lax.dot_general(
                weights,
                jnp.concatenate([upper, under, upper], 0),
                NN,
                preferred_element_type=jnp.float32,
            )
            rounded[side * half_count + index] = value.astype(jnp.bfloat16)
            return 0

        lax.fori_loop(0, half_count, make_basis, 0, unroll=8)

    order = rounded.shape[1]
    columns = lax.broadcasted_iota(jnp.int32, (order, left.shape[1]), 1)

    def row_and_column(packed):
        return (packed >> 8) & 255, packed & 255

    near_copy.wait()

    def near_step(step, _):
        values = []
        for inner in range(4):
            at = step * 4 + inner
            row, column = row_and_column(slots_ref[slots + at])
            value = lax.dot_general(rounded[column], near[at], NT, preferred_element_type=jnp.float32)
            values.append((row, value))
        for row, value in values:
            total[row // group, row % group] += value
        return 0

    lax.fori_loop(0, near.shape[0] // 4, near_step, 0)

    def slot_step(step, _):
        coefs = []
        for inner in range(UNROLL):
            at = step * UNROLL + inner
            packed = slots_ref[at]
            row, column = row_and_column(packed)
            coef = lax.dot_general(rounded[column], right[at], NT, preferred_element_type=jnp.float32)
            coef = jnp.where(columns < (packed >> 16), coef, 0.0).astype(jnp.bfloat16)
            coefs.append((row, coef))
        values = []
        for inner, (row, coef) in enumerate(coefs):
            value = lax.dot_general(
                coef, left[step * UNROLL + inner], NN, preferred_element_type=jnp.float32
            )
            values.append((row, value))
        for row, value in values:
            total[row // group, row % group] += value
        return 0

    for chunk in range(CHUNKS):
        for copy in copies[chunk]:
            copy.wait()
        lax.fori_loop(chunk * per // UNROLL, (chunk + 1) * per // UNROLL, slot_step, 0)
    terms_ref[...] = total[...].astype(terms_ref.dtype)


def apply_operator(prepare, small_count, grams, halves, operator, terms_shape, terms_dtype):
    slots, near, left, right = operator
    group, order, leaf = terms_shape[1:]
    clusters = 2 * (halves[0].shape[0] - 1)
    panels = len(halves) // 2
    square = jax.ShapeDtypeStruct((order, order), jnp.float32)
    return pl.pallas_call(
        functools.partial(apply_kernel, prepare, len(grams), small_count, panels),
        out_shape=(
            *[square] * small_count,
            jax.ShapeDtypeStruct((group, order, leaf), jnp.float32),
            jax.ShapeDtypeStruct(terms_shape, terms_dtype),
        ),
        in_specs=[smem()]
        + [vmem()] * (len(grams) + len(halves))
        + [pl.BlockSpec(memory_space=pl.ANY)] * 3,
        out_specs=tuple(vmem() for _ in range(small_count + 2)),
        scratch_shapes=[
            pltpu.VMEM(terms_shape, jnp.float32),
            pltpu.VMEM((clusters, order, leaf), jnp.bfloat16),
            pltpu.VMEM(near.shape, near.dtype),
            pltpu.VMEM(left.shape, left.dtype),
            pltpu.VMEM(right.shape, right.dtype),
            pltpu.SemaphoreType.DMA((CHUNKS, 2)),
            pltpu.SemaphoreType.DMA,
        ],
        compiler_params=pltpu.CompilerParams(vmem_limit_bytes=VMEM_LIMIT),
    )(slots, *grams, *halves, near, left, right)


def call(kernel, outs, *operands, specs=None):
    return pl.pallas_call(
        kernel,
        out_shape=tuple(jax.ShapeDtypeStruct(shape, jnp.float32) for shape in outs),
        in_specs=specs or [vmem()] * len(operands),
        out_specs=tuple(vmem() for _ in outs),
        compiler_params=pltpu.CompilerParams(vmem_limit_bytes=VMEM_LIMIT),
    )(*operands)


def exchange(values, axis, distance):
    count = lax.axis_size(axis)
    return lax.ppermute(values, axis, [(at, at ^ distance) for at in range(count)])


SEG_STEPS = ("seg", (1, 2, 3))
CHIP_STEPS = ("rows", (2, 4, 6))


def reduce_rows_seg(values):
    for axis, steps in (SEG_STEPS, CHIP_STEPS):
        one, two, three = [exchange(values, axis, step) for step in steps]
        values = (values + one) + (two + three)
    return values + exchange(values, "rows", 1)


def gather_halves(message):
    for axis, steps in (SEG_STEPS, CHIP_STEPS):
        merged = (4 * (message.shape[0] - 1) + 1,) + message.shape[1:]
        (message,) = call(merge_kernel, [merged], message, *[exchange(message, axis, step) for step in steps])
    return [message, exchange(message, "rows", 1)]


def spread_cols(values):
    count = lax.axis_size("cols")
    return lax.all_to_all(jnp.broadcast_to(values[None], (count,) + values.shape), "cols", 0, 0)


def body(
    right_side,
    near_blocks,
    near_rows,
    near_cols,
    left_factors,
    right_factors,
    slot_ranks,
    slot_rows,
    slot_cols,
):
    col_count = lax.axis_size("cols")
    col_index = lax.axis_index("cols")
    order, cells = right_side.shape
    leaf = near_blocks.shape[-1]
    group = cells // leaf // col_count
    me = lax.axis_index("rows") * lax.axis_size("seg") + lax.axis_index("seg")

    def packed(ranks, rows, columns):
        piece = (columns // group) ^ me
        place = ((piece >> 3) & 3) * 4 + ((piece >> 2) & 1) * 16 + (piece & 3)
        return ranks * 65536 + rows * 256 + place * group + columns % group

    operator = (
        jnp.concatenate(
            [
                packed(slot_ranks.reshape(-1), slot_rows.reshape(-1), slot_cols.reshape(-1)),
                packed(0, near_rows.reshape(-1), near_cols.reshape(-1)),
            ]
        ),
        near_blocks.reshape(near_blocks.shape[3:]),
        left_factors.reshape(left_factors.shape[3:]),
        right_factors.reshape(right_factors.shape[3:]),
    )
    share_shape = (group, order, leaf)
    message_shape = (group + 1, order, leaf)
    terms_shape = (col_count,) + share_shape

    (message,) = call(
        start_kernel, [message_shape], col_index.reshape(1), right_side, specs=[smem(), vmem()]
    )
    start_halves = gather_halves(message)
    start_factor, base, first_share, terms = apply_operator(
        start_mixes, 2, start_halves, start_halves, operator, terms_shape, jnp.float32
    )
    received = lax.all_to_all(terms, "cols", 0, 0)
    (share,) = call(sum_kernel, [share_shape], received)
    image_piece = spread_cols(share)
    (message,) = call(first_image_kernel, [message_shape], base, right_side, image_piece, share)
    image_halves = gather_halves(message)
    head, lower, top_inverse, own, mix, second_share, terms = apply_operator(
        middle_mixes,
        5,
        [*image_halves, base],
        image_halves + start_halves,
        operator,
        terms_shape,
        jnp.bfloat16,
    )
    received = lax.all_to_all(terms, "cols", 0, 0)
    (gram,) = call(
        second_image_kernel,
        [(order + order // 2, 2 * order)],
        first_share,
        second_share,
        received,
    )
    grams = spread_cols(reduce_rows_seg(gram))
    answer, hessen = call(
        final_kernel,
        [(order, cells), (3 * order, 2 * order)],
        grams,
        start_factor,
        head,
        lower,
        top_inverse,
        own,
        mix,
        base,
        right_side,
        image_piece,
    )
    return (answer, hessen)


def solution(mesh):
    in_specs = (
        P(None, ("rows", "seg")),
        P("rows", "seg", "cols", None, None, None),
        P("rows", "seg", "cols", None),
        P("rows", "seg", "cols", None),
        P("rows", "seg", "cols", None, None, None),
        P("rows", "seg", "cols", None, None, None),
        P("rows", "seg", "cols", None),
        P("rows", "seg", "cols", None),
        P("rows", "seg", "cols", None),
    )
    out_specs = (P(None, ("rows", "seg")), P())
    return jax.shard_map(body, mesh=mesh, in_specs=in_specs, out_specs=out_specs, check_vma=False)
```

```python
import functools

import jax
import jax.numpy as jnp
from jax import lax
from jax.experimental import pallas as pl
from jax.experimental.pallas import tpu as pltpu
from jax.sharding import PartitionSpec as P

FULL = lax.Precision.HIGHEST
NN = (((1,), (0,)), ((), ()))
NT = (((1,), (1,)), ((), ()))
TN = (((0,), (0,)), ((), ()))
CHUNKS = 4
UNROLL = 64
VMEM_LIMIT = 48 * 1024 * 1024


def mm(a, b, dims=NN):
    return lax.dot_general(a, b, dims, precision=FULL, preferred_element_type=jnp.float32)


def vmem():
    return pl.BlockSpec(memory_space=pltpu.VMEM)


def smem():
    return pl.BlockSpec(memory_space=pltpu.SMEM)


def eye(order):
    rows = lax.broadcasted_iota(jnp.int32, (order, order), 0)
    cols = lax.broadcasted_iota(jnp.int32, (order, order), 1)
    return (rows == cols).astype(jnp.float32)


def eliminate(works):
    order = works[0].shape[0]
    groups = [[work[at : at + 8] for at in range(0, order, 8)] for work in works]
    places = lax.broadcasted_iota(jnp.int32, groups[0][0].shape, 0)

    def lane(value, at):
        return jnp.broadcast_to(value[:, at : at + 1], value.shape)

    def pivots(parts, base):
        head = parts[base // 8]
        rows = [jnp.broadcast_to(head[at : at + 1], head.shape) for at in range(8)]
        corner = [[lane(row, base + at) for at in range(8)] for row in rows]
        steps, ratios, scaled = [], [], []
        for at in range(8):
            inverse = 1.0 / corner[at][at]
            ratio = {later: corner[at][later] * inverse for later in range(at + 1, 8)}
            steps.append(rows[at] * inverse)
            ratios.append(ratio)
            scaled.append(rows[at] * (1.0 / jnp.sqrt(corner[at][at])))
            for later in range(at + 1, 8):
                rows[later] = rows[later] - ratio[later] * rows[at]
                for column in range(later, 8):
                    corner[later][column] = corner[later][column] - ratio[later] * corner[at][column]
        result = scaled[0]
        for at in range(1, 8):
            result = jnp.where(places == at, scaled[at], result)
        return result, steps, ratios

    for base in range(0, order, 8):
        for parts in groups:
            parts[base // 8], steps, ratios = pivots(parts, base)
            for below in range(base // 8 + 1, len(parts)):
                value = parts[below]
                factors = [lane(value, base + at) for at in range(8)]
                for at in range(8):
                    for earlier in range(at):
                        factors[at] = factors[at] - ratios[earlier][at] * factors[earlier]
                for at in range(8):
                    value = value - factors[at] * steps[at]
                parts[below] = value
    results = []
    for parts in groups:
        work = jnp.concatenate(parts, 0)
        rows = lax.broadcasted_iota(jnp.int32, work.shape, 0)
        cols = lax.broadcasted_iota(jnp.int32, work.shape, 1)
        results.append(jnp.where(cols >= rows, work, 0.0))
    return results


def split(value):
    high = value.astype(jnp.bfloat16)
    return high, (value - high.astype(jnp.float32)).astype(jnp.bfloat16)


def sum_leading(ref):
    total = ref[0]
    for index in range(1, ref.shape[0]):
        total = total + ref[index].astype(jnp.float32)
    return total


def start_kernel(column_ref, piece_ref, message_ref):
    piece = piece_ref[...]
    group, leaf = message_ref.shape[0] - 1, message_ref.shape[2]
    for half in range(group):
        first = pl.multiple_of((column_ref[0] * group + half) * leaf, leaf)
        message_ref[half] = piece_ref[:, pl.ds(first, leaf)]
    gram = mm(piece, piece, NT)
    message_ref[group] = jnp.concatenate([gram, jnp.zeros_like(gram)], 1)


def share_products(bases, share):
    group = len(share)
    products = []
    for base in bases + [share]:
        total = mm(base[0], share[0], NT)
        for half in range(1, group):
            total = total + mm(base[half], share[half], NT)
        products.append(total)
    return products


def in_cells(ref):
    parts = [ref[at, half] for at in range(ref.shape[0]) for half in range(ref.shape[1])]
    return jnp.concatenate(parts, 1)


def sum_kernel(terms_ref, share_ref):
    share_ref[...] = sum_leading(terms_ref)


def first_image_kernel(base_ref, right_ref, image_ref, share_ref, message_ref):
    basis = mm(base_ref[...], right_ref[...])
    image = in_cells(image_ref)
    order, group = image.shape[0], share_ref.shape[0]
    products = mm(jnp.concatenate([basis, image], 0), image, NT)
    message_ref[:group] = share_ref[...]
    message_ref[group] = jnp.concatenate([products[:order], products[order:]], 1)


def second_image_kernel(first_ref, second_ref, terms_ref, gram_ref):
    total = terms_ref[0].astype(jnp.float32)
    for index in range(1, terms_ref.shape[0]):
        total = total + terms_ref[index].astype(jnp.float32)
    group, order = total.shape[0], total.shape[1]
    share = [total[half] for half in range(group)]
    bases = [[ref[half] for half in range(group)] for ref in (first_ref, second_ref)]
    one, two, square = share_products(bases, share)
    gram_ref[:order] = jnp.concatenate([one, two], 1)
    gram_ref[order:] = jnp.concatenate([square[: order // 2], square[order // 2 :]], 1)


def merge_kernel(own_ref, one_ref, two_ref, three_ref, out_ref):
    refs = (own_ref, one_ref, two_ref, three_ref)
    count = own_ref.shape[0] - 1
    for at, ref in enumerate(refs):
        out_ref[at * count : (at + 1) * count] = ref[:count]
    out_ref[4 * count] = (own_ref[count] + one_ref[count]) + (two_ref[count] + three_ref[count])


def final_kernel(
    grams_ref,
    start_ref,
    head_ref,
    lower_ref,
    top_inverse_ref,
    own_ref,
    mix_ref,
    base_ref,
    right_ref,
    image_ref,
    out_ref,
    hessen_ref,
):
    totals = sum_leading(grams_ref)
    order = start_ref.shape[0]
    unit = eye(order)
    cross_one = totals[:order, :order]
    inner = totals[:order, order:]
    square = jnp.concatenate([totals[order:, :order], totals[order:, order:]], 0)
    cross_two = inner + 0.5 * unit
    gram = square - mm(cross_one, cross_one, TN) - mm(inner, inner, TN)
    start, head, lower = start_ref[...], head_ref[...], lower_ref[...]
    top_inverse = top_inverse_ref[...]
    side = mm(head, cross_one, TN) + mm(lower, cross_two, TN)
    corner = mm(cross_one, cross_one, TN) + mm(cross_two, cross_two, TN) + gram
    bridge = mm(top_inverse, side)
    part = mm(top_inverse, mm(head, start, TN))
    schur = corner - mm(bridge, bridge, TN)
    rest = mm(cross_one, start, TN) - mm(bridge, part, TN)
    schur_done, gram_done = eliminate(
        [jnp.concatenate([schur, unit], 1), jnp.concatenate([gram, rest], 1)]
    )
    low_inverse = schur_done[:, order:]
    low_weights = mm(low_inverse, mm(low_inverse, rest), TN)
    top_weights = mm(top_inverse, part - mm(bridge, low_weights), TN)
    hessen_ref[:order, :] = jnp.concatenate([head, cross_one], 1)
    hessen_ref[order : 2 * order, :] = jnp.concatenate([lower, cross_two], 1)
    hessen_ref[2 * order :, :] = jnp.concatenate([jnp.zeros_like(head), gram_done[:, :order]], 1)
    for_image = mm(low_weights, own_ref[...], TN)
    for_right = mm(top_weights, base_ref[...], TN) + mm(low_weights, mix_ref[...], TN)
    weights = jnp.concatenate([for_right, for_image], 1)
    out_ref[...] = mm(weights, jnp.concatenate([right_ref[...], in_cells(image_ref)], 0))


def start_mixes(gram_refs, out_refs):
    last = gram_refs[0].shape[0] - 1
    totals = gram_refs[0][last] + gram_refs[1][last]
    order = totals.shape[0]
    (done,) = eliminate([jnp.concatenate([totals[:, :order], eye(order)], 1)])
    factor_ref, base_ref = out_refs
    factor_ref[...] = done[:, :order]
    base_ref[...] = done[:, order:]
    return [done[:, order:]]


def middle_mixes(gram_refs, out_refs):
    last = gram_refs[0].shape[0] - 1
    totals = gram_refs[0][last] + gram_refs[1][last]
    base = gram_refs[2][...]
    order = totals.shape[0]
    unit = eye(order)
    cross, square = totals[:, :order], totals[:, order:]
    gram = square - mm(cross, cross, TN)
    head = cross + 0.5 * unit
    top = mm(head, head, TN) + gram
    done, top_done = eliminate(
        [jnp.concatenate([gram, unit], 1), jnp.concatenate([top, unit], 1)]
    )
    own = done[:, order:]
    mix = -mm(mm(own, cross, NT), base)
    head_ref, lower_ref, top_inverse_ref, own_ref, mix_ref = out_refs
    head_ref[...] = head
    lower_ref[...] = done[:, :order]
    top_inverse_ref[...] = top_done[:, order:]
    own_ref[...] = own
    mix_ref[...] = mix
    return [own, mix]


def apply_kernel(prepare, gram_count, out_count, panels, slots_ref, *refs):
    gram_refs, refs = refs[:gram_count], refs[gram_count:]
    panel_refs, refs = refs[: 2 * panels], refs[2 * panels :]
    near_hbm, left_hbm, right_hbm = refs[:3]
    small_outs, refs = refs[3 : 3 + out_count], refs[3 + out_count :]
    basis_ref, terms_ref = refs[:2]
    total, rounded, near, left, right, sems, near_sem = refs[2:]
    slots = left.shape[0]
    per = slots // CHUNKS
    near_copy = pltpu.make_async_copy(near_hbm, near, near_sem)
    near_copy.start()
    copies = []
    for chunk in range(CHUNKS):
        part = pl.ds(chunk * per, per)
        pair = (
            pltpu.make_async_copy(right_hbm.at[part], right.at[part], sems.at[chunk, 0]),
            pltpu.make_async_copy(left_hbm.at[part], left.at[part], sems.at[chunk, 1]),
        )
        for copy in pair:
            copy.start()
        copies.append(pair)
    total[...] = jnp.zeros_like(total)
    mixes = prepare(gram_refs, small_outs)
    group = total.shape[1]
    for half in range(group):
        share = mm(mixes[0], panel_refs[0][half])
        for at in range(1, panels):
            share = share + mm(mixes[at], panel_refs[2 * at][half])
        basis_ref[half] = share
    high, low = split(jnp.concatenate(mixes, 1))
    weights = jnp.concatenate([high, high, low], 1)
    half_count = rounded.shape[0] // 2
    for side in range(2):

        def make_basis(index, _, side=side):
            stacked = jnp.concatenate([panel_refs[2 * at + side][index] for at in range(panels)], 0)
            upper, under = split(stacked)
            value = lax.dot_general(
                weights,
                jnp.concatenate([upper, under, upper], 0),
                NN,
                preferred_element_type=jnp.float32,
            )
            rounded[side * half_count + index] = value.astype(jnp.bfloat16)
            return 0

        lax.fori_loop(0, half_count, make_basis, 0, unroll=8)

    order = rounded.shape[1]
    columns = lax.broadcasted_iota(jnp.int32, (order, left.shape[1]), 1)

    def row_and_column(packed):
        return (packed >> 8) & 255, packed & 255

    near_copy.wait()

    def near_step(step, _):
        values = []
        for inner in range(4):
            at = step * 4 + inner
            row, column = row_and_column(slots_ref[slots + at])
            value = lax.dot_general(rounded[column], near[at], NT, preferred_element_type=jnp.float32)
            values.append((row, value))
        for row, value in values:
            total[row // group, row % group] += value
        return 0

    lax.fori_loop(0, near.shape[0] // 4, near_step, 0)

    def slot_step(step, _):
        coefs = []
        for inner in range(UNROLL):
            at = step * UNROLL + inner
            packed = slots_ref[at]
            row, column = row_and_column(packed)
            coef = lax.dot_general(rounded[column], right[at], NT, preferred_element_type=jnp.float32)
            coef = jnp.where(columns < (packed >> 16), coef, 0.0).astype(jnp.bfloat16)
            coefs.append((row, coef))
        values = []
        for inner, (row, coef) in enumerate(coefs):
            value = lax.dot_general(
                coef, left[step * UNROLL + inner], NN, preferred_element_type=jnp.float32
            )
            values.append((row, value))
        for row, value in values:
            total[row // group, row % group] += value
        return 0

    for chunk in range(CHUNKS):
        for copy in copies[chunk]:
            copy.wait()
        lax.fori_loop(chunk * per // UNROLL, (chunk + 1) * per // UNROLL, slot_step, 0)
    terms_ref[...] = total[...].astype(terms_ref.dtype)


def apply_operator(prepare, small_count, grams, halves, operator, terms_shape, terms_dtype):
    slots, near, left, right = operator
    group, order, leaf = terms_shape[1:]
    clusters = 2 * (halves[0].shape[0] - 1)
    panels = len(halves) // 2
    square = jax.ShapeDtypeStruct((order, order), jnp.float32)
    return pl.pallas_call(
        functools.partial(apply_kernel, prepare, len(grams), small_count, panels),
        out_shape=(
            *[square] * small_count,
            jax.ShapeDtypeStruct((group, order, leaf), jnp.float32),
            jax.ShapeDtypeStruct(terms_shape, terms_dtype),
        ),
        in_specs=[smem()]
        + [vmem()] * (len(grams) + len(halves))
        + [pl.BlockSpec(memory_space=pl.ANY)] * 3,
        out_specs=tuple(vmem() for _ in range(small_count + 2)),
        scratch_shapes=[
            pltpu.VMEM(terms_shape, jnp.float32),
            pltpu.VMEM((clusters, order, leaf), jnp.bfloat16),
            pltpu.VMEM(near.shape, near.dtype),
            pltpu.VMEM(left.shape, left.dtype),
            pltpu.VMEM(right.shape, right.dtype),
            pltpu.SemaphoreType.DMA((CHUNKS, 2)),
            pltpu.SemaphoreType.DMA,
        ],
        compiler_params=pltpu.CompilerParams(vmem_limit_bytes=VMEM_LIMIT),
    )(slots, *grams, *halves, near, left, right)


def call(kernel, outs, *operands, specs=None):
    return pl.pallas_call(
        kernel,
        out_shape=tuple(jax.ShapeDtypeStruct(shape, jnp.float32) for shape in outs),
        in_specs=specs or [vmem()] * len(operands),
        out_specs=tuple(vmem() for _ in outs),
        compiler_params=pltpu.CompilerParams(vmem_limit_bytes=VMEM_LIMIT),
    )(*operands)


def exchange(values, axis, distance):
    count = lax.axis_size(axis)
    return lax.ppermute(values, axis, [(at, at ^ distance) for at in range(count)])


SEG_STEPS = ("seg", (1, 2, 3))
CHIP_STEPS = ("rows", (2, 4, 6))


def reduce_rows_seg(values):
    for axis, steps in (SEG_STEPS, CHIP_STEPS):
        one, two, three = [exchange(values, axis, step) for step in steps]
        values = (values + one) + (two + three)
    return values + exchange(values, "rows", 1)


def gather_halves(message):
    for axis, steps in (SEG_STEPS, CHIP_STEPS):
        merged = (4 * (message.shape[0] - 1) + 1,) + message.shape[1:]
        (message,) = call(merge_kernel, [merged], message, *[exchange(message, axis, step) for step in steps])
    return [message, exchange(message, "rows", 1)]


def spread_cols(values):
    count = lax.axis_size("cols")
    return lax.all_to_all(jnp.broadcast_to(values[None], (count,) + values.shape), "cols", 0, 0)


def body(
    right_side,
    near_blocks,
    near_rows,
    near_cols,
    left_factors,
    right_factors,
    slot_ranks,
    slot_rows,
    slot_cols,
):
    col_count = lax.axis_size("cols")
    col_index = lax.axis_index("cols")
    order, cells = right_side.shape
    leaf = near_blocks.shape[-1]
    group = cells // leaf // col_count
    me = lax.axis_index("rows") * lax.axis_size("seg") + lax.axis_index("seg")

    def packed(ranks, rows, columns):
        piece = (columns // group) ^ me
        place = ((piece >> 3) & 3) * 4 + ((piece >> 2) & 1) * 16 + (piece & 3)
        return ranks * 65536 + rows * 256 + place * group + columns % group

    operator = (
        jnp.concatenate(
            [
                packed(slot_ranks.reshape(-1), slot_rows.reshape(-1), slot_cols.reshape(-1)),
                packed(0, near_rows.reshape(-1), near_cols.reshape(-1)),
            ]
        ),
        near_blocks.reshape(near_blocks.shape[3:]),
        left_factors.reshape(left_factors.shape[3:]),
        right_factors.reshape(right_factors.shape[3:]),
    )
    share_shape = (group, order, leaf)
    message_shape = (group + 1, order, leaf)
    terms_shape = (col_count,) + share_shape

    (message,) = call(
        start_kernel, [message_shape], col_index.reshape(1), right_side, specs=[smem(), vmem()]
    )
    start_halves = gather_halves(message)
    start_factor, base, first_share, terms = apply_operator(
        start_mixes, 2, start_halves, start_halves, operator, terms_shape, jnp.float32
    )
    received = lax.all_to_all(terms, "cols", 0, 0)
    (share,) = call(sum_kernel, [share_shape], received)
    image_piece = spread_cols(share)
    (message,) = call(first_image_kernel, [message_shape], base, right_side, image_piece, share)
    image_halves = gather_halves(message)
    head, lower, top_inverse, own, mix, second_share, terms = apply_operator(
        middle_mixes,
        5,
        [*image_halves, base],
        image_halves + start_halves,
        operator,
        terms_shape,
        jnp.bfloat16,
    )
    received = lax.all_to_all(terms, "cols", 0, 0)
    (gram,) = call(
        second_image_kernel,
        [(order + order // 2, 2 * order)],
        first_share,
        second_share,
        received,
    )
    grams = spread_cols(reduce_rows_seg(gram))
    answer, hessen = call(
        final_kernel,
        [(order, cells), (3 * order, 2 * order)],
        grams,
        start_factor,
        head,
        lower,
        top_inverse,
        own,
        mix,
        base,
        right_side,
        image_piece,
    )
    return (answer, hessen)


def solution(mesh):
    in_specs = (
        P(None, ("rows", "seg")),
        P("rows", "seg", "cols", None, None, None),
        P("rows", "seg", "cols", None),
        P("rows", "seg", "cols", None),
        P("rows", "seg", "cols", None, None, None),
        P("rows", "seg", "cols", None, None, None),
        P("rows", "seg", "cols", None),
        P("rows", "seg", "cols", None),
        P("rows", "seg", "cols", None),
    )
    out_specs = (P(None, ("rows", "seg")), P())
    return jax.shard_map(body, mesh=mesh, in_specs=in_specs, out_specs=out_specs, check_vma=False)
```

```python
import functools

import jax
import jax.numpy as jnp
from jax import lax
from jax.experimental import pallas as pl
from jax.experimental.pallas import tpu as pltpu
from jax.sharding import PartitionSpec as P

FULL = lax.Precision.HIGHEST
NN = (((1,), (0,)), ((), ()))
NT = (((1,), (1,)), ((), ()))
TN = (((0,), (0,)), ((), ()))
CHUNKS = 4
UNROLL = 64
VMEM_LIMIT = 48 * 1024 * 1024


def mm(a, b, dims=NN):
    return lax.dot_general(a, b, dims, precision=FULL, preferred_element_type=jnp.float32)


def vmem():
    return pl.BlockSpec(memory_space=pltpu.VMEM)


def smem():
    return pl.BlockSpec(memory_space=pltpu.SMEM)


def eye(order):
    rows = lax.broadcasted_iota(jnp.int32, (order, order), 0)
    cols = lax.broadcasted_iota(jnp.int32, (order, order), 1)
    return (rows == cols).astype(jnp.float32)


def eliminate(works):
    order = works[0].shape[0]
    groups = [[work[at : at + 8] for at in range(0, order, 8)] for work in works]
    places = lax.broadcasted_iota(jnp.int32, groups[0][0].shape, 0)

    def lane(value, at):
        return jnp.broadcast_to(value[:, at : at + 1], value.shape)

    def pivots(parts, base):
        head = parts[base // 8]
        rows = [jnp.broadcast_to(head[at : at + 1], head.shape) for at in range(8)]
        corner = [[lane(row, base + at) for at in range(8)] for row in rows]
        steps, ratios, scaled = [], [], []
        for at in range(8):
            inverse = 1.0 / corner[at][at]
            ratio = {later: corner[at][later] * inverse for later in range(at + 1, 8)}
            steps.append(rows[at] * inverse)
            ratios.append(ratio)
            scaled.append(rows[at] * (1.0 / jnp.sqrt(corner[at][at])))
            for later in range(at + 1, 8):
                rows[later] = rows[later] - ratio[later] * rows[at]
                for column in range(later, 8):
                    corner[later][column] = corner[later][column] - ratio[later] * corner[at][column]
        result = scaled[0]
        for at in range(1, 8):
            result = jnp.where(places == at, scaled[at], result)
        return result, steps, ratios

    for base in range(0, order, 8):
        for parts in groups:
            parts[base // 8], steps, ratios = pivots(parts, base)
            for below in range(base // 8 + 1, len(parts)):
                value = parts[below]
                factors = [lane(value, base + at) for at in range(8)]
                for at in range(8):
                    for earlier in range(at):
                        factors[at] = factors[at] - ratios[earlier][at] * factors[earlier]
                for at in range(8):
                    value = value - factors[at] * steps[at]
                parts[below] = value
    results = []
    for parts in groups:
        work = jnp.concatenate(parts, 0)
        rows = lax.broadcasted_iota(jnp.int32, work.shape, 0)
        cols = lax.broadcasted_iota(jnp.int32, work.shape, 1)
        results.append(jnp.where(cols >= rows, work, 0.0))
    return results


def split(value):
    high = value.astype(jnp.bfloat16)
    return high, (value - high.astype(jnp.float32)).astype(jnp.bfloat16)


def sum_leading(ref):
    total = ref[0]
    for index in range(1, ref.shape[0]):
        total = total + ref[index].astype(jnp.float32)
    return total


def start_kernel(column_ref, piece_ref, message_ref):
    piece = piece_ref[...]
    group, leaf = message_ref.shape[0] - 1, message_ref.shape[2]
    for half in range(group):
        first = pl.multiple_of((column_ref[0] * group + half) * leaf, leaf)
        message_ref[half] = piece_ref[:, pl.ds(first, leaf)]
    gram = mm(piece, piece, NT)
    message_ref[group] = jnp.concatenate([gram, jnp.zeros_like(gram)], 1)


def share_products(bases, share):
    group = len(share)
    products = []
    for base in bases + [share]:
        total = mm(base[0], share[0], NT)
        for half in range(1, group):
            total = total + mm(base[half], share[half], NT)
        products.append(total)
    return products


def in_cells(ref):
    parts = [ref[at, half] for at in range(ref.shape[0]) for half in range(ref.shape[1])]
    return jnp.concatenate(parts, 1)


def sum_kernel(terms_ref, share_ref, spread_ref):
    total = sum_leading(terms_ref)
    share_ref[...] = total
    for at in range(spread_ref.shape[0]):
        spread_ref[at] = total


def first_image_kernel(base_ref, right_ref, image_ref, share_ref, message_ref):
    basis = mm(base_ref[...], right_ref[...])
    image = in_cells(image_ref)
    order, group = image.shape[0], share_ref.shape[0]
    products = mm(jnp.concatenate([basis, image], 0), image, NT)
    message_ref[:group] = share_ref[...]
    message_ref[group] = jnp.concatenate([products[:order], products[order:]], 1)


def second_image_kernel(first_ref, second_ref, terms_ref, gram_ref):
    total = terms_ref[0].astype(jnp.float32)
    for index in range(1, terms_ref.shape[0]):
        total = total + terms_ref[index].astype(jnp.float32)
    group, order = total.shape[0], total.shape[1]
    share = [total[half] for half in range(group)]
    bases = [[ref[half] for half in range(group)] for ref in (first_ref, second_ref)]
    one, two, square = share_products(bases, share)
    gram_ref[:order] = jnp.concatenate([one, two], 1)
    gram_ref[order:] = jnp.concatenate([square[: order // 2], square[order // 2 :]], 1)


def merge_kernel(own_ref, one_ref, two_ref, three_ref, out_ref):
    refs = (own_ref, one_ref, two_ref, three_ref)
    count = own_ref.shape[0] - 1
    for at, ref in enumerate(refs):
        out_ref[at * count : (at + 1) * count] = ref[:count]
    out_ref[4 * count] = (own_ref[count] + one_ref[count]) + (two_ref[count] + three_ref[count])


def final_kernel(
    grams_ref,
    start_ref,
    head_ref,
    lower_ref,
    top_inverse_ref,
    own_ref,
    mix_ref,
    base_ref,
    right_ref,
    image_ref,
    out_ref,
    hessen_ref,
):
    totals = sum_leading(grams_ref)
    order = start_ref.shape[0]
    unit = eye(order)
    cross_one = totals[:order, :order]
    inner = totals[:order, order:]
    square = jnp.concatenate([totals[order:, :order], totals[order:, order:]], 0)
    cross_two = inner + 0.5 * unit
    gram = square - mm(cross_one, cross_one, TN) - mm(inner, inner, TN)
    start, head, lower = start_ref[...], head_ref[...], lower_ref[...]
    top_inverse = top_inverse_ref[...]
    side = mm(head, cross_one, TN) + mm(lower, cross_two, TN)
    corner = mm(cross_one, cross_one, TN) + mm(cross_two, cross_two, TN) + gram
    bridge = mm(top_inverse, side)
    part = mm(top_inverse, mm(head, start, TN))
    schur = corner - mm(bridge, bridge, TN)
    rest = mm(cross_one, start, TN) - mm(bridge, part, TN)
    schur_done, gram_done = eliminate(
        [jnp.concatenate([schur, unit], 1), jnp.concatenate([gram, rest], 1)]
    )
    low_inverse = schur_done[:, order:]
    low_weights = mm(low_inverse, mm(low_inverse, rest), TN)
    top_weights = mm(top_inverse, part - mm(bridge, low_weights), TN)
    hessen_ref[:order, :] = jnp.concatenate([head, cross_one], 1)
    hessen_ref[order : 2 * order, :] = jnp.concatenate([lower, cross_two], 1)
    hessen_ref[2 * order :, :] = jnp.concatenate([jnp.zeros_like(head), gram_done[:, :order]], 1)
    for_image = mm(low_weights, own_ref[...], TN)
    for_right = mm(top_weights, base_ref[...], TN) + mm(low_weights, mix_ref[...], TN)
    weights = jnp.concatenate([for_right, for_image], 1)
    out_ref[...] = mm(weights, jnp.concatenate([right_ref[...], in_cells(image_ref)], 0))


def start_mixes(gram_refs, out_refs):
    last = gram_refs[0].shape[0] - 1
    totals = gram_refs[0][last] + gram_refs[1][last]
    order = totals.shape[0]
    (done,) = eliminate([jnp.concatenate([totals[:, :order], eye(order)], 1)])
    factor_ref, base_ref = out_refs
    factor_ref[...] = done[:, :order]
    base_ref[...] = done[:, order:]
    return [done[:, order:]]


def middle_mixes(gram_refs, out_refs):
    last = gram_refs[0].shape[0] - 1
    totals = gram_refs[0][last] + gram_refs[1][last]
    base = gram_refs[2][...]
    order = totals.shape[0]
    unit = eye(order)
    cross, square = totals[:, :order], totals[:, order:]
    gram = square - mm(cross, cross, TN)
    head = cross + 0.5 * unit
    top = mm(head, head, TN) + gram
    done, top_done = eliminate(
        [jnp.concatenate([gram, unit], 1), jnp.concatenate([top, unit], 1)]
    )
    own = done[:, order:]
    mix = -mm(mm(own, cross, NT), base)
    head_ref, lower_ref, top_inverse_ref, own_ref, mix_ref = out_refs
    head_ref[...] = head
    lower_ref[...] = done[:, :order]
    top_inverse_ref[...] = top_done[:, order:]
    own_ref[...] = own
    mix_ref[...] = mix
    return [own, mix]


def apply_kernel(prepare, gram_count, out_count, panels, slots_ref, *refs):
    gram_refs, refs = refs[:gram_count], refs[gram_count:]
    panel_refs, refs = refs[: 2 * panels], refs[2 * panels :]
    near_hbm, left_hbm, right_hbm = refs[:3]
    small_outs, refs = refs[3 : 3 + out_count], refs[3 + out_count :]
    basis_ref, terms_ref = refs[:2]
    total, rounded, near, left, right, sems, near_sem = refs[2:]
    slots = left.shape[0]
    per = slots // CHUNKS
    near_copy = pltpu.make_async_copy(near_hbm, near, near_sem)
    near_copy.start()
    copies = []
    for chunk in range(CHUNKS):
        part = pl.ds(chunk * per, per)
        pair = (
            pltpu.make_async_copy(right_hbm.at[part], right.at[part], sems.at[chunk, 0]),
            pltpu.make_async_copy(left_hbm.at[part], left.at[part], sems.at[chunk, 1]),
        )
        for copy in pair:
            copy.start()
        copies.append(pair)
    total[...] = jnp.zeros_like(total)
    mixes = prepare(gram_refs, small_outs)
    group = total.shape[1]
    for half in range(group):
        share = mm(mixes[0], panel_refs[0][half])
        for at in range(1, panels):
            share = share + mm(mixes[at], panel_refs[2 * at][half])
        basis_ref[half] = share
    high, low = split(jnp.concatenate(mixes, 1))
    weights = jnp.concatenate([high, high, low], 1)
    half_count = rounded.shape[0] // 2
    for side in range(2):

        def make_basis(index, _, side=side):
            stacked = jnp.concatenate([panel_refs[2 * at + side][index] for at in range(panels)], 0)
            upper, under = split(stacked)
            value = lax.dot_general(
                weights,
                jnp.concatenate([upper, under, upper], 0),
                NN,
                preferred_element_type=jnp.float32,
            )
            rounded[side * half_count + index] = value.astype(jnp.bfloat16)
            return 0

        lax.fori_loop(0, half_count, make_basis, 0, unroll=32)

    order = rounded.shape[1]
    columns = lax.broadcasted_iota(jnp.int32, (order, left.shape[1]), 1)

    def row_and_column(packed):
        return (packed >> 8) & 255, packed & 255

    near_copy.wait()

    def near_step(step, _):
        values = []
        for inner in range(16):
            at = step * 16 + inner
            row, column = row_and_column(slots_ref[slots + at])
            value = lax.dot_general(rounded[column], near[at], NT, preferred_element_type=jnp.float32)
            values.append((row, value))
        for row, value in values:
            total[row // group, row % group] += value
        return 0

    lax.fori_loop(0, near.shape[0] // 16, near_step, 0)

    def slot_step(step, _):
        coefs = []
        for inner in range(UNROLL):
            at = step * UNROLL + inner
            packed = slots_ref[at]
            row, column = row_and_column(packed)
            coef = lax.dot_general(rounded[column], right[at], NT, preferred_element_type=jnp.float32)
            coef = jnp.where(columns < (packed >> 16), coef, 0.0).astype(jnp.bfloat16)
            coefs.append((row, coef))
        values = []
        for inner, (row, coef) in enumerate(coefs):
            value = lax.dot_general(
                coef, left[step * UNROLL + inner], NN, preferred_element_type=jnp.float32
            )
            values.append((row, value))
        for row, value in values:
            total[row // group, row % group] += value
        return 0

    for chunk in range(CHUNKS):
        for copy in copies[chunk]:
            copy.wait()
        lax.fori_loop(chunk * per // UNROLL, (chunk + 1) * per // UNROLL, slot_step, 0)
    terms_ref[...] = total[...].astype(terms_ref.dtype)


def apply_operator(prepare, small_count, grams, halves, operator, terms_shape, terms_dtype):
    slots, near, left, right = operator
    group, order, leaf = terms_shape[1:]
    clusters = 2 * (halves[0].shape[0] - 1)
    panels = len(halves) // 2
    square = jax.ShapeDtypeStruct((order, order), jnp.float32)
    return pl.pallas_call(
        functools.partial(apply_kernel, prepare, len(grams), small_count, panels),
        out_shape=(
            *[square] * small_count,
            jax.ShapeDtypeStruct((group, order, leaf), jnp.float32),
            jax.ShapeDtypeStruct(terms_shape, terms_dtype),
        ),
        in_specs=[smem()]
        + [vmem()] * (len(grams) + len(halves))
        + [pl.BlockSpec(memory_space=pl.ANY)] * 3,
        out_specs=tuple(vmem() for _ in range(small_count + 2)),
        scratch_shapes=[
            pltpu.VMEM(terms_shape, jnp.float32),
            pltpu.VMEM((clusters, order, leaf), jnp.bfloat16),
            pltpu.VMEM(near.shape, near.dtype),
            pltpu.VMEM(left.shape, left.dtype),
            pltpu.VMEM(right.shape, right.dtype),
            pltpu.SemaphoreType.DMA((CHUNKS, 2)),
            pltpu.SemaphoreType.DMA,
        ],
        compiler_params=pltpu.CompilerParams(vmem_limit_bytes=VMEM_LIMIT),
    )(slots, *grams, *halves, near, left, right)


def call(kernel, outs, *operands, specs=None):
    return pl.pallas_call(
        kernel,
        out_shape=tuple(jax.ShapeDtypeStruct(shape, jnp.float32) for shape in outs),
        in_specs=specs or [vmem()] * len(operands),
        out_specs=tuple(vmem() for _ in outs),
        compiler_params=pltpu.CompilerParams(vmem_limit_bytes=VMEM_LIMIT),
    )(*operands)


def exchange(values, axis, distance):
    count = lax.axis_size(axis)
    return lax.ppermute(values, axis, [(at, at ^ distance) for at in range(count)])


SEG_STEPS = ("seg", (1, 2, 3))
CHIP_STEPS = ("rows", (2, 4, 6))


def reduce_rows_seg(values):
    for axis, steps in (SEG_STEPS, CHIP_STEPS):
        one, two, three = [exchange(values, axis, step) for step in steps]
        values = (values + one) + (two + three)
    return values + exchange(values, "rows", 1)


def gather_halves(message):
    for axis, steps in (SEG_STEPS, CHIP_STEPS):
        merged = (4 * (message.shape[0] - 1) + 1,) + message.shape[1:]
        (message,) = call(merge_kernel, [merged], message, *[exchange(message, axis, step) for step in steps])
    return [message, exchange(message, "rows", 1)]


def spread_cols(values):
    count = lax.axis_size("cols")
    return lax.all_to_all(jnp.broadcast_to(values[None], (count,) + values.shape), "cols", 0, 0)


def body(
    right_side,
    near_blocks,
    near_rows,
    near_cols,
    left_factors,
    right_factors,
    slot_ranks,
    slot_rows,
    slot_cols,
):
    col_count = lax.axis_size("cols")
    col_index = lax.axis_index("cols")
    order, cells = right_side.shape
    leaf = near_blocks.shape[-1]
    group = cells // leaf // col_count
    me = lax.axis_index("rows") * lax.axis_size("seg") + lax.axis_index("seg")

    def packed(ranks, rows, columns):
        piece = (columns // group) ^ me
        place = ((piece >> 3) & 3) * 4 + ((piece >> 2) & 1) * 16 + (piece & 3)
        return ranks * 65536 + rows * 256 + place * group + columns % group

    operator = (
        jnp.concatenate(
            [
                packed(slot_ranks.reshape(-1), slot_rows.reshape(-1), slot_cols.reshape(-1)),
                packed(0, near_rows.reshape(-1), near_cols.reshape(-1)),
            ]
        ),
        near_blocks.reshape(near_blocks.shape[3:]),
        left_factors.reshape(left_factors.shape[3:]),
        right_factors.reshape(right_factors.shape[3:]),
    )
    share_shape = (group, order, leaf)
    message_shape = (group + 1, order, leaf)
    terms_shape = (col_count,) + share_shape

    (message,) = call(
        start_kernel, [message_shape], col_index.reshape(1), right_side, specs=[smem(), vmem()]
    )
    start_halves = gather_halves(message)
    start_factor, base, first_share, terms = apply_operator(
        start_mixes, 2, start_halves, start_halves, operator, terms_shape, jnp.float32
    )
    received = lax.all_to_all(terms, "cols", 0, 0)
    share, spread = call(sum_kernel, [share_shape, terms_shape], received)
    image_piece = lax.all_to_all(spread, "cols", 0, 0)
    (message,) = call(first_image_kernel, [message_shape], base, right_side, image_piece, share)
    image_halves = gather_halves(message)
    head, lower, top_inverse, own, mix, second_share, terms = apply_operator(
        middle_mixes,
        5,
        [*image_halves, base],
        image_halves + start_halves,
        operator,
        terms_shape,
        jnp.bfloat16,
    )
    received = lax.all_to_all(terms, "cols", 0, 0)
    (gram,) = call(
        second_image_kernel,
        [(order + order // 2, 2 * order)],
        first_share,
        second_share,
        received,
    )
    grams = spread_cols(reduce_rows_seg(gram))
    answer, hessen = call(
        final_kernel,
        [(order, cells), (3 * order, 2 * order)],
        grams,
        start_factor,
        head,
        lower,
        top_inverse,
        own,
        mix,
        base,
        right_side,
        image_piece,
    )
    return (answer, hessen)


def solution(mesh):
    in_specs = (
        P(None, ("rows", "seg")),
        P("rows", "seg", "cols", None, None, None),
        P("rows", "seg", "cols", None),
        P("rows", "seg", "cols", None),
        P("rows", "seg", "cols", None, None, None),
        P("rows", "seg", "cols", None, None, None),
        P("rows", "seg", "cols", None),
        P("rows", "seg", "cols", None),
        P("rows", "seg", "cols", None),
    )
    out_specs = (P(None, ("rows", "seg")), P())
    return jax.shard_map(body, mesh=mesh, in_specs=in_specs, out_specs=out_specs, check_vma=False)
```
